256 devices in a mesh: clip: 128 (over y, z, x_lo, core), row: 2 (over x_hi).
Axes of the slice: x: 4 (x_hi: 2, x_lo: 2; x = x_hi * 2 + x_lo), y: 4, z: 8, core: 2. Of those that a mesh axis runs over, the one named last changes fastest.
Arguments:
- video: bfloat16 [2048, 2, 64, 1280], P('clip', 'row'), may hold values from -6 to 6
- frame_pick: int32 [128], P('clip'), may hold values from 0 to 15
- w_query: bfloat16 [1280, 640], replicated, as said below
- w_key: bfloat16 [1280, 640], replicated, may hold values from -0.15625 to 0.15625
- w_value: bfloat16 [1280, 640], replicated, may hold values from -0.15625 to 0.15625
- w_out: bfloat16 [640, 1280], replicated, may hold values from -0.25 to 0.25
Outputs:
- mixed: bfloat16 [2048, 2, 64, 1280], P('clip', 'row')
The draws below stay inside these ranges and needn't reach their ends.
Inputs may be any that keep to these rules, and one draw needn't show every extreme that they name: `w_query`: A query projection with columns of independent entries. `frame_pick`: A frame index within a clip.
All inputs are finite; a program needn't handle non-finite values.
Results may differ from the reference program's by a relative error of at most 0.0059.
The reference program's roundings to bfloat16 on the way (of `normed`, `query`, `glob_keys`, `probs` and `attended`) count: a program that leaves them out, or rounds other values in their place, can miss the bound.
Values may be sent and summed in bfloat16 or wider, within the bound.
No kernel may reach another device: no remote copies, remote signals or barrier semaphores. Data moves between devices by JAX's collectives and lax.ppermute only.
A program may use at most 128 MiB of HBM per device.

```python
import math
import jax
import jax.numpy as jnp
from jax import lax

D = 1280
H = 10
HD = 64
FR = 16
CTX = 16
COLS = 64
HQ = 640
HALF = 32
FRAMES = 2048
LROWS = 2
N_CLIP = 128


def draw_w_query(key, part):
    key = jax.random.fold_in(key, 7)
    first = jax.random.fold_in(key, 0)
    base = jax.random.normal(first, (D, H * HD), jnp.float32) * D ** (-0.5)
    return base.astype(jnp.bfloat16)


def set_ends(entries, own_key, low, high):
    longest = entries.shape.index(max(entries.shape))
    spots = []
    for shift in (0, 1):
        where = [jax.random.randint(jax.random.fold_in(own_key, axis), (), 0, length) for axis, length in enumerate(entries.shape)]
        where[longest] = (where[longest] + shift) % entries.shape[longest]
        spots.append(tuple(where))
    return entries.at[spots[0]].set(low).at[spots[1]].set(high)


def level_of(key, shape, cuts, low, top_value):
    def one(axis_at, blocks):
        draws = jax.random.uniform(jax.random.fold_in(jax.random.fold_in(key, 6), axis_at), (blocks,), jnp.float32, low / len(cuts), top_value / len(cuts))
        return jnp.repeat(jnp.exp(draws), shape[axis_at] // blocks).reshape((-1,) + (1,) * (len(shape) - axis_at - 1))

    loudness = one(*cuts[0])
    for cut in cuts[1:]:
        loudness = loudness * one(*cut)
    return loudness


def normal_values(rng, shape, scale, reach, cuts=(), kind=jnp.bfloat16):
    level = level_of(rng, shape, cuts, -0.22, 0.18) if cuts else 1.0
    array = jax.random.normal(rng, shape, jnp.float32) * scale * level
    return jnp.minimum(jnp.maximum(array, -reach), reach).astype(kind)


def setup_inputs(seed: int = 0) -> dict:
    seeds = jax.random.split(jax.random.key(seed), 7)
    video = normal_values(seeds[0], (FRAMES, LROWS, COLS, D), 1.0, 6.0, ((0, 128), (1, 2)))
    frame_pick = set_ends(jax.random.randint(seeds[1], (N_CLIP,), 0, FR), jax.random.fold_in(seeds[1], 1), 0, FR - 1).astype(jnp.int32)
    w_query = draw_w_query(jax.random.fold_in(seeds[6], 71), 0)
    w_key = normal_values(seeds[3], (D, HQ), D ** -0.5, 0.15625)
    w_value = normal_values(seeds[4], (D, HQ), D ** -0.5, 0.15625)
    w_out = normal_values(seeds[5], (HQ, D), HQ ** -0.5, 0.25)
    return dict(video=video, frame_pick=frame_pick, w_query=w_query, w_key=w_key, w_value=w_value, w_out=w_out)


def normalize(values):
    centre = values - lax.optimization_barrier(jnp.mean(values, -1, keepdims=True))
    spread = lax.optimization_barrier(jnp.mean(centre * centre, -1, keepdims=True))
    return centre * lax.rsqrt(spread + 1e-05)

def reference(video, frame_pick, w_query, w_key, w_value, w_out):
    width = video.shape[-1]
    blocks = video.reshape(N_CLIP, FR, LROWS, COLS, width)

    def prepare(block):
        normed = normalize(block.astype(jnp.float32)).astype(jnp.bfloat16)
        flat = normed.reshape(-1, width)
        query = jnp.dot(flat, w_query, preferred_element_type=jnp.float32).astype(jnp.bfloat16)
        keys = jnp.dot(flat, w_key, preferred_element_type=jnp.float32).astype(jnp.bfloat16)
        values = jnp.dot(flat, w_value, preferred_element_type=jnp.float32).astype(jnp.bfloat16)
        return (normed, query, keys, values)
    normed, query, keys, values = lax.map(prepare, blocks)
    chosen = normed[jnp.arange(N_CLIP), frame_pick].astype(jnp.float32)
    chosen = lax.optimization_barrier(jnp.sum(chosen, axis=1)).reshape(N_CLIP, HALF, 2, width)
    chosen = lax.optimization_barrier(jnp.sum(chosen, axis=2))
    pooled = lax.optimization_barrier(jnp.sum(chosen.reshape(CTX, N_CLIP // CTX, HALF, width), axis=1))
    glob = normalize(pooled).astype(jnp.bfloat16).reshape(-1, width)
    glob_keys = jnp.dot(glob, w_key, preferred_element_type=jnp.float32).astype(jnp.bfloat16)
    glob_values = jnp.dot(glob, w_value, preferred_element_type=jnp.float32).astype(jnp.bfloat16)

    def spread_out(table):
        table = jnp.repeat(table.reshape(CTX, HALF, H, HD), 2, axis=1)
        return jnp.broadcast_to(table[:, None], (CTX, LROWS, COLS, H, HD))
    glob_keys = spread_out(glob_keys)
    glob_values = spread_out(glob_values)
    pad_spec = ((2, 2), (0, 0), (0, 0), (0, 0))
    keys_pad = jnp.pad(keys.reshape(FRAMES, LROWS, COLS, HQ), pad_spec)
    values_pad = jnp.pad(values.reshape(FRAMES, LROWS, COLS, HQ), pad_spec)
    scale = 1.0 / math.sqrt(HD)

    def attend(item):
        clip_id, block, clip_query = item
        start = (clip_id * FR).astype(jnp.int32)
        near_keys = lax.dynamic_slice_in_dim(keys_pad, start, FR + 4, 0).reshape(FR + 4, LROWS, COLS, H, HD)
        near_values = lax.dynamic_slice_in_dim(values_pad, start, FR + 4, 0).reshape(FR + 4, LROWS, COLS, H, HD)
        all_keys = jnp.concatenate([near_keys, glob_keys], 0).astype(jnp.float32)
        all_values = jnp.concatenate([near_values, glob_values], 0).astype(jnp.float32)
        q_five = clip_query.reshape(FR, LROWS, COLS, H, HD).astype(jnp.float32)
        scores = jnp.einsum('frchd,grchd->rchfg', q_five, all_keys) * scale
        slot = jnp.arange(FR + 4 + CTX)
        valid = ((slot >= 2) | (clip_id > 0)) & ((slot < FR + 2) | (slot >= FR + 4) | (clip_id < N_CLIP - 1))
        scores = jnp.where(valid, scores, -jnp.inf)
        top = lax.optimization_barrier(jnp.max(scores, -1, keepdims=True))
        expo = jnp.exp(scores - top)
        probs = (expo / lax.optimization_barrier(jnp.sum(expo, -1, keepdims=True))).astype(jnp.bfloat16)
        attended = jnp.einsum('rchfg,grchd->frchd', probs.astype(jnp.float32), all_values)
        attended = attended.astype(jnp.bfloat16).reshape(-1, HQ)
        update = jnp.dot(attended, w_out, preferred_element_type=jnp.float32)
        mixed = block.astype(jnp.float32).reshape(-1, width) + update
        return mixed.astype(jnp.bfloat16).reshape(FR, LROWS, COLS, width)
    mixed = lax.map(attend, (jnp.arange(N_CLIP, dtype=jnp.int32), blocks, query))
    return mixed.reshape(FRAMES, LROWS, COLS, width)
```

```python
import functools
import math

import jax
import jax.numpy as jnp
from jax import lax
from jax.experimental import pallas as pl
from jax.experimental.pallas import tpu as pltpu
from jax.sharding import PartitionSpec as P

HD = 64
GC = 8
AXES = ("clip", "row")
BIG = -1e30
F32 = jnp.float32
BF16 = jnp.bfloat16


def place(i):
    clip, xh = divmod(i, 2)
    return (clip >> 5, (clip >> 2) & 7, xh * 2 + ((clip >> 1) & 1), clip & 1)


def index(y, z, x, core):
    clip = ((y * 8 + z) * 2 + (x & 1)) * 2 + core
    return clip * 2 + (x >> 1)


def send(value, move):
    pairs = [(i, index(*move(*place(i)))) for i in range(256)]
    return lax.ppermute(value, AXES, pairs)


def layer_norm(values):
    centre = values - jnp.mean(values, -1, keepdims=True)
    spread = jnp.mean(centre * centre, -1, keepdims=True)
    return centre * lax.rsqrt(spread + 1e-05)


def my_place():
    clip = lax.axis_index("clip")
    return lax.axis_index("row") * 2 + lax.rem(clip // 2, 2), lax.rem(clip, 2)


def pick_kernel(pick_ref, video_ref, keep_ref, give_ref):
    x, core = my_place()
    normed = layer_norm(video_ref[0, 0].astype(F32)).astype(BF16)
    row = lax.broadcasted_iota(jnp.int32, (32, 64), 0)
    column = lax.broadcasted_iota(jnp.int32, (32, 64), 1)
    half = jnp.where(row < 16, core, 1 - core)
    quarter = ((row // 4) % 4 + x) % 4
    pooled = half * 16 + quarter * 4 + row % 4
    pairs = jnp.where(column // 2 == pooled, 1.0, 0.0).astype(BF16)
    term = jnp.dot(pairs, normed, preferred_element_type=F32)
    keep_ref[...] = term[:16]
    give_ref[...] = term[16:]


def pick(video, frame_pick):
    width = video.shape[-1]
    half = jax.ShapeDtypeStruct((16, width), F32)
    whole = pl.BlockSpec((16, width), lambda i, p: (0, 0))
    return pl.pallas_call(
        pick_kernel,
        grid_spec=pltpu.PrefetchScalarGridSpec(
            num_scalar_prefetch=1,
            grid=(1,),
            in_specs=[pl.BlockSpec((1, 1, 64, width), lambda i, p: (p[0], 0, 0, 0))],
            out_specs=[whole, whole],
        ),
        out_shape=[half, half],
        name="pick",
    )(frame_pick, video)


def split_kernel(keep_ref, came_ref, *out_refs):
    total = keep_ref[...] + came_ref[...]
    for s, out in enumerate(out_refs):
        out[...] = total[4 * s : 4 * s + 4]


def split(keep, came):
    part = jax.ShapeDtypeStruct((4, keep.shape[1]), F32)
    return pl.pallas_call(split_kernel, out_shape=[part] * 4, name="split")(keep, came)


def sum_kernel(a_ref, b_ref, c_ref, d_ref, out_ref):
    out_ref[...] = (a_ref[...] + b_ref[...]) + (c_ref[...] + d_ref[...])


def total_of(parts):
    return pl.pallas_call(
        sum_kernel, out_shape=jax.ShapeDtypeStruct(parts[0].shape, F32), name="total"
    )(*parts)


def glob_kernel(a_ref, b_ref, out_ref):
    out_ref[...] = layer_norm(a_ref[...] + b_ref[...]).astype(BF16)


def glob_of(a, b):
    return pl.pallas_call(
        glob_kernel, out_shape=jax.ShapeDtypeStruct(a.shape, BF16), name="glob"
    )(a, b)


def project_kernel(glob_ref, wk_ref, wv_ref, out_ref):
    glob = glob_ref[...]
    features = wk_ref.shape[1]
    out_ref[:, :features] = jnp.dot(glob, wk_ref[...], preferred_element_type=F32).astype(BF16)
    out_ref[:, features:] = jnp.dot(glob, wv_ref[...], preferred_element_type=F32).astype(BF16)


def project(glob, w_key, w_value):
    rows, width = glob.shape
    features = w_key.shape[1]
    return pl.pallas_call(
        project_kernel,
        out_shape=jax.ShapeDtypeStruct((rows, 2 * features), BF16),
        compiler_params=pltpu.CompilerParams(vmem_limit_bytes=16 << 20),
        name="project",
    )(glob, w_key, w_value)


def qkv_kernel(video_ref, wq_ref, wk_ref, wv_ref, q_ref, kv_ref, near_ref, far_ref):
    _, core = my_place()
    width = video_ref.shape[-1]
    features = wq_ref.shape[1]
    normed = layer_norm(video_ref[:, 0].astype(F32))
    normed = jnp.concatenate([normed[:, :GC].reshape(-1, width), normed[:, GC:].reshape(-1, width)], 0)
    normed = normed.astype(BF16)
    query = jnp.dot(normed, wq_ref[...], preferred_element_type=F32).astype(BF16)
    keys = jnp.dot(normed, wk_ref[...], preferred_element_type=F32).astype(BF16)
    values = jnp.dot(normed, wv_ref[...], preferred_element_type=F32).astype(BF16)
    q_ref[...] = query.reshape(q_ref.shape)
    kv_ref[:, :, :features] = keys.reshape(2, -1, features)
    kv_ref[:, :, features:] = values.reshape(2, -1, features)
    last = kv_ref.shape[1] - 2 * GC
    head = kv_ref[:, : 2 * GC]
    tail = kv_ref[:, last:]
    even = core == 0
    near_ref[...] = jnp.where(even, tail, head)
    far_ref[...] = jnp.where(even, head, tail)


def qkv(video, w_query, w_key, w_value):
    frames, _, columns, width = video.shape
    features = w_query.shape[1]
    groups = columns // GC
    whole = lambda w: pl.BlockSpec(w.shape, lambda i: (0, 0))
    block = lambda rows, wide: pl.BlockSpec((2, rows, wide), lambda i: (i, 0, 0))
    shape = lambda rows, wide: jax.ShapeDtypeStruct((groups, rows, wide), BF16)
    sizes = [(frames * GC, features), (frames * GC, 2 * features), (2 * GC, 2 * features), (2 * GC, 2 * features)]
    return pl.pallas_call(
        qkv_kernel,
        grid=(columns // 16,),
        in_specs=[
            pl.BlockSpec((frames, 1, 16, width), lambda i: (0, 0, i, 0)),
            whole(w_query),
            whole(w_key),
            whole(w_value),
        ],
        out_specs=[block(*s) for s in sizes],
        out_shape=[shape(*s) for s in sizes],
        compiler_params=pltpu.CompilerParams(vmem_limit_bytes=48 << 20),
        cost_estimate=pl.CostEstimate(
            flops=2 * frames * columns * width * 3 * features, bytes_accessed=14 << 20, transcendentals=0
        ),
        name="qkv",
    )(video, w_query, w_key, w_value)


def attend_kernel(video_ref, q_ref, kv_ref, near_ref, far_ref, own_ref, other_ref, wo_ref, out_ref):
    frames = video_ref.shape[0]
    width = video_ref.shape[-1]
    features = q_ref.shape[-1]
    rows = frames * GC
    local = rows + 4 * GC
    total = local + 64
    step = pl.program_id(0)
    x, core = my_place()
    clip = lax.axis_index("clip")
    alone = (clip == 0) | (clip == lax.axis_size("clip") - 1)

    lane = lax.broadcasted_iota(jnp.int32, (1, 128), 1)
    low = lane < HD
    spot = lax.broadcasted_iota(jnp.int32, (total, 128), 1) % HD
    key = lax.broadcasted_iota(jnp.int32, (total, 128), 0)
    match = jnp.where(key < local, key % GC, (key - local) % 4) == jnp.where(key < local, spot, spot // 2)
    absent = (key >= local - 2 * GC) & (key < local) & alone
    bad = ((spot < GC) & jnp.logical_not(match)) | ((spot == GC) & absent)
    key_mask = jnp.where(bad, BIG, 0.0).astype(BF16)
    q_spot = lax.broadcasted_iota(jnp.int32, (rows, 128), 1) % HD
    q_row = lax.broadcasted_iota(jnp.int32, (rows, 128), 0)
    query_mask = jnp.where((q_spot == q_row % GC) | (q_spot == GC), 1.0, 0.0).astype(BF16)
    scale = math.log2(math.e) / math.sqrt(HD)

    mixed = []
    for g in range(2):
        group = step * 2 + g
        mine = group // 4 == core
        shift = lax.rem(group - x + 8, 4)
        blocks = []
        for hp in range(features // 128):
            lanes = slice(hp * 128, hp * 128 + 128)
            late = slice(features + hp * 128, features + hp * 128 + 128)

            def gathered(at):
                glob = jnp.where(mine, own_ref[shift, :, at], other_ref[shift, :, at])
                return jnp.concatenate([kv_ref[g, :, at], near_ref[g, :, at], far_ref[g, :, at], glob], 0)

            query = q_ref[g, :, lanes]
            keys = gathered(lanes)
            values = gathered(late)
            parts = []
            for first in (True, False):
                here = low if first else jnp.logical_not(low)
                scores = lax.dot_general(
                    jnp.where(here, query, query_mask),
                    jnp.where(here, keys, key_mask),
                    (((1,), (1,)), ((), ())),
                    preferred_element_type=F32,
                )
                top = jnp.max(scores, -1, keepdims=True)
                weights = jnp.exp2((scores - top) * scale).astype(BF16)
                parts.append(
                    jnp.dot(weights, jnp.where(here, values, jnp.ones_like(values)), preferred_element_type=F32)
                )
            sums = jnp.where(low, parts[1], parts[0])
            blocks.append((jnp.where(low, parts[0], parts[1]) / pltpu.roll(sums, HD, 1)).astype(BF16))
        mixed.append(jnp.concatenate(blocks, 1))
    update = jnp.dot(jnp.concatenate(mixed, 0), wo_ref[...], preferred_element_type=F32)
    update = update.reshape(2, frames, GC, width)
    update = jnp.concatenate([update[0], update[1]], 1)
    out_ref[:, 0] = (video_ref[:, 0].astype(F32) + update).astype(BF16)


def attend(video, q, kv, near, far, own, other, w_out):
    frames, _, columns, width = video.shape
    features = q.shape[-1]
    video_spec = pl.BlockSpec((frames, 1, 16, width), lambda i: (0, 0, i, 0))
    block = lambda a: pl.BlockSpec((2,) + a.shape[1:], lambda i: (i, 0, 0))
    whole = lambda a: pl.BlockSpec(a.shape, lambda i: (0,) * a.ndim)
    return pl.pallas_call(
        attend_kernel,
        grid=(columns // 16,),
        in_specs=[
            video_spec,
            block(q),
            block(kv),
            block(near),
            block(far),
            whole(own),
            whole(other),
            whole(w_out),
        ],
        out_specs=video_spec,
        out_shape=jax.ShapeDtypeStruct(video.shape, BF16),
        compiler_params=pltpu.CompilerParams(vmem_limit_bytes=48 << 20),
        cost_estimate=pl.CostEstimate(flops=6 << 30, bytes_accessed=14 << 20, transcendentals=0),
        name="attend",
    )(video, q, kv, near, far, own, other, w_out)


def far_z(z):
    return {0: 6, 6: 0, 1: 7, 7: 1, 2: 4, 4: 2, 3: 5, 5: 3}[z]


def halo_far(value):
    count = lax.axis_size("clip")
    pairs = []
    for c in range(1, count - 1, 2):
        pairs += [(c, c + 1), (c + 1, c)]
    return lax.ppermute(value, "clip", pairs)


def local(video, frame_pick, w_query, w_key, w_value, w_out):
    width = video.shape[-1]
    keep, give = pick(video, frame_pick)
    came = send(give, lambda y, z, x, c: (y, z, x, 1 - c))
    parts = split(keep, came)
    arrived = [send(parts[s], lambda y, z, x, c, s=s: (y, z, (x + s) % 4, c)) for s in (1, 2, 3)]
    term = total_of([parts[0]] + arrived)
    glob = glob_of(term, send(term, lambda y, z, x, c: (y, z ^ 1, x, c)))
    for move in (
        lambda y, z, x, c: (y, z ^ 2, x, c),
        lambda y, z, x, c: (y, far_z(z), x, c),
        lambda y, z, x, c: (y ^ 1, z, x, c),
        lambda y, z, x, c: (3 - y, z, x, c),
    ):
        glob = jnp.concatenate([glob, send(glob, move)], 0)
    piece = project(glob, w_key, w_value)
    ring = [send(piece, lambda y, z, x, c, s=s: (y, z, (x - s) % 4, c)) for s in (1, 2, 3)]
    own = jnp.stack([piece] + ring)
    other = send(own, lambda y, z, x, c: (y, z, x, 1 - c))

    q, kv, near, far = qkv(video, w_query, w_key, w_value)
    near = send(near, lambda y, z, x, c: (y, z, x, 1 - c))
    far = halo_far(far)
    return attend(video, q, kv, near, far, own, other, w_out)


def solution(mesh):
    placed = (P("clip", "row", None, None), P("clip"), P(), P(), P(), P())
    return jax.shard_map(
        local, mesh=mesh, in_specs=placed, out_specs=P("clip", "row", None, None), check_vma=False
    )
```

```python
import functools
import math

import jax
import jax.numpy as jnp
from jax import lax
from jax.experimental import pallas as pl
from jax.experimental.pallas import tpu as pltpu
from jax.sharding import PartitionSpec as P

HD = 64
GC = 8
AXES = ("clip", "row")
BIG = -1e30
F32 = jnp.float32
BF16 = jnp.bfloat16


def place(i):
    clip, xh = divmod(i, 2)
    return (clip >> 5, (clip >> 2) & 7, xh * 2 + ((clip >> 1) & 1), clip & 1)


def index(y, z, x, core):
    clip = ((y * 8 + z) * 2 + (x & 1)) * 2 + core
    return clip * 2 + (x >> 1)


def send(value, move):
    pairs = [(i, index(*move(*place(i)))) for i in range(256)]
    return lax.ppermute(value, AXES, pairs)


def layer_norm(values):
    centre = values - jnp.mean(values, -1, keepdims=True)
    spread = jnp.mean(centre * centre, -1, keepdims=True)
    return centre * lax.rsqrt(spread + 1e-05)


def my_place():
    clip = lax.axis_index("clip")
    return lax.axis_index("row") * 2 + lax.rem(clip // 2, 2), lax.rem(clip, 2)


VMEM = pl.BlockSpec(memory_space=pltpu.VMEM)
ANY = pl.BlockSpec(memory_space=pl.ANY)


def call(kernel, out_shape, name, operands, after=(), aliases=None, limit=16, flops=0):
    count = len(operands)

    def body(*refs):
        kernel(*refs[:count], *refs[count + len(after) :])

    single = not isinstance(out_shape, (list, tuple))
    return pl.pallas_call(
        body,
        in_specs=[VMEM] * count + [ANY] * len(after),
        out_specs=VMEM if single else [VMEM] * len(out_shape),
        out_shape=out_shape,
        input_output_aliases=aliases or {},
        compiler_params=pltpu.CompilerParams(vmem_limit_bytes=limit << 20),
        cost_estimate=pl.CostEstimate(flops=flops, bytes_accessed=1 << 14, transcendentals=0),
        name=name,
    )(*operands, *after)


def pick_kernel(pick_ref, video_ref, keep_ref, give_ref):
    x, core = my_place()
    normed = layer_norm(video_ref[0, 0].astype(F32)).astype(BF16)
    row = lax.broadcasted_iota(jnp.int32, (32, 64), 0)
    column = lax.broadcasted_iota(jnp.int32, (32, 64), 1)
    half = jnp.where(row < 16, core, 1 - core)
    quarter = ((row // 4) % 4) ^ x
    pooled = half * 16 + quarter * 4 + row % 4
    pairs = jnp.where(column // 2 == pooled, 1.0, 0.0).astype(BF16)
    term = jnp.dot(pairs, normed, preferred_element_type=F32)
    keep_ref[...] = term[:16]
    give_ref[...] = term[16:]


def pick(video, frame_pick):
    width = video.shape[-1]
    half = jax.ShapeDtypeStruct((16, width), F32)
    return pl.pallas_call(
        pick_kernel,
        grid_spec=pltpu.PrefetchScalarGridSpec(
            num_scalar_prefetch=1,
            grid=(1,),
            in_specs=[pl.BlockSpec((1, 1, 64, width), lambda i, p: (p[0], 0, 0, 0))],
            out_specs=[VMEM, VMEM],
        ),
        out_shape=[half, half],
        compiler_params=pltpu.CompilerParams(vmem_limit_bytes=16 << 20),
        name="pick",
    )(frame_pick, video)


def split_kernel(keep_ref, came_ref, *out_refs):
    total = keep_ref[...] + came_ref[...]
    for s, out in enumerate(out_refs):
        out[...] = total[4 * s : 4 * s + 4]


def sum_kernel(a_ref, b_ref, c_ref, d_ref, out_ref):
    out_ref[...] = (a_ref[...] + b_ref[...]) + (c_ref[...] + d_ref[...])


def glob_kernel(a_ref, b_ref, out_ref):
    out_ref[0] = layer_norm(a_ref[...] + b_ref[...]).astype(BF16)


def stack_kernel(*refs):
    out_ref = refs[-1]
    at = 0
    for ref in refs[:-1]:
        out_ref[at : at + ref.shape[0]] = ref[...]
        at += ref.shape[0]


def project_kernel(*refs):
    globs, (wk_ref, wv_ref, out_ref) = refs[:-3], refs[-3:]
    glob = jnp.concatenate([ref[i].astype(F32) for ref in globs for i in range(ref.shape[0])], 0).astype(BF16)
    features = wk_ref.shape[1]
    out_ref[0, :, :features] = jnp.dot(glob, wk_ref[...], preferred_element_type=F32).astype(BF16)
    out_ref[0, :, features:] = jnp.dot(glob, wv_ref[...], preferred_element_type=F32).astype(BF16)


def qkv_kernel(part, *refs):
    video_ref, wq_ref, wk_ref, wv_ref = refs[:4]
    q_ref, kv_ref, near_ref, far_ref = refs[-4:]
    _, core = my_place()
    width = video_ref.shape[-1]
    features = wq_ref.shape[1]
    normed = layer_norm(video_ref[:, 0, part * 16 : part * 16 + 16].astype(F32))
    normed = jnp.concatenate([normed[:, :GC].reshape(-1, width), normed[:, GC:].reshape(-1, width)], 0)
    normed = normed.astype(BF16)
    rows = normed.shape[0] // 2
    mine = slice(2 * part, 2 * part + 2)
    query = jnp.dot(normed, wq_ref[...], preferred_element_type=F32).astype(BF16)
    q_ref[mine] = query.reshape(2, rows, features)
    even = core == 0
    for at, w_ref in ((slice(0, features), wk_ref), (slice(features, 2 * features), wv_ref)):
        made = jnp.dot(normed, w_ref[...], preferred_element_type=F32).astype(BF16).reshape(2, rows, features)
        kv_ref[mine, :, at] = made
        first, last = made[:, : 2 * GC], made[:, rows - 2 * GC :]
        near_ref[mine, :, at] = jnp.where(even, last, first)
        far_ref[mine, :, at] = jnp.where(even, first, last)


def qkv(part, video, weights, made, after):
    frames, _, columns, width = video.shape
    features = weights[0].shape[1]
    groups = columns // GC
    sizes = [(frames * GC, features), (frames * GC, 2 * features), (2 * GC, 2 * features), (2 * GC, 2 * features)]
    return call(
        functools.partial(qkv_kernel, part),
        [jax.ShapeDtypeStruct((groups,) + s, BF16) for s in sizes],
        "qkv",
        [video, *weights, *made],
        after,
        {4 + i: i for i in range(len(made))},
        flops=2 * frames * 16 * width * 3 * features,
    )


LAG, LATE = 3, 2
SCALE = math.log2(math.e) / math.sqrt(HD)


def queries_mask(rows):
    spot = lax.broadcasted_iota(jnp.int32, (rows, 128), 1) % HD
    row = lax.broadcasted_iota(jnp.int32, (rows, 128), 0)
    return jnp.where((spot == row % GC) | (spot == GC), 1.0, 0.0).astype(BF16)


def keys_mask(plain, pooled, absent):
    spot = lax.broadcasted_iota(jnp.int32, (plain + pooled, 128), 1) % HD
    row = lax.broadcasted_iota(jnp.int32, (plain + pooled, 128), 0)
    same = row % GC == spot
    if pooled:
        same = (same & (row < plain)) | ((row % 4 == spot // 2) & (row >= plain))
    bad = (spot < GC) & jnp.logical_not(same)
    if absent is not None:
        bad = bad | ((spot == GC) & absent(row))
    return jnp.where(bad, BIG, 0.0).astype(BF16)


def scores_of(here, keys, key_mask, query, query_mask):
    return lax.dot_general(
        jnp.where(here, keys, key_mask),
        jnp.where(here, query, query_mask),
        (((1,), (1,)), ((), ())),
        preferred_element_type=F32,
    )


def near_kernel(groups, *refs):
    q_ref, kv_ref = refs[:2]
    sums_ref, stats_ref = refs[-2:]
    rows, features = q_ref.shape[1:]
    low = lax.broadcasted_iota(jnp.int32, (1, 128), 1) < HD
    key_mask, query_mask = keys_mask(rows, 0, None), queries_mask(rows)
    units = [(g, hp, i) for g in groups for hp in range(features // 128) for i in range(2)]
    scores, weights, loaded = {}, {}, {}
    for t in range(len(units) + LAG + LATE):
        if t < len(units):
            g, hp, i = units[t]
            if i == 0:
                lanes = slice(hp * 128, hp * 128 + 128)
                late = slice(features + hp * 128, features + hp * 128 + 128)
                loaded[g, hp] = q_ref[g, :, lanes], kv_ref[g, :, lanes], kv_ref[g, :, late].T
            query, keys, _ = loaded[g, hp]
            here = low if i == 0 else jnp.logical_not(low)
            scores[t] = scores_of(here, keys, key_mask, query, query_mask)
        if 0 <= t - LAG < len(units):
            g, hp, i = units[t - LAG]
            score = scores.pop(t - LAG)
            top = jnp.max(score, 0, keepdims=True)
            weight = jnp.exp2((score - top) * SCALE)
            head = 2 * hp + i
            stats_ref[g, 0, head : head + 1] = top
            stats_ref[g, 1, head : head + 1] = jnp.sum(weight, 0, keepdims=True)
            weights[t - LAG] = weight.astype(BF16)
        if t >= LAG + LATE:
            g, hp, i = units[t - LAG - LATE]
            head = 2 * hp + i
            values = loaded[g, hp][2][i * HD : i * HD + HD]
            sums_ref[g, head * HD : head * HD + HD] = jnp.dot(
                values, weights.pop(t - LAG - LATE), preferred_element_type=F32
            )


def near_part(groups, q, kv, made, after):
    count, rows, features = q.shape
    return call(
        functools.partial(near_kernel, groups),
        [
            jax.ShapeDtypeStruct((count, features, rows), F32),
            jax.ShapeDtypeStruct((count, 2, 16, rows), F32),
        ],
        "near",
        [q, kv, *made],
        after,
        {2 + i: i for i in range(len(made))},
        flops=len(groups) * 300 << 20,
    )


def finish_kernel(video_ref, q_ref, sums_ref, stats_ref, near_ref, far_ref, own_ref, other_ref, wo_ref, out_ref):
    frames = video_ref.shape[0]
    width = video_ref.shape[-1]
    rows, features = q_ref.shape[1:]
    step = pl.program_id(0)
    x, core = my_place()
    clip = lax.axis_index("clip")
    alone = (clip == 0) | (clip == lax.axis_size("clip") - 1)
    low = lax.broadcasted_iota(jnp.int32, (1, 128), 1) < HD
    key_mask = keys_mask(4 * GC, 64, lambda row: (row >= 2 * GC) & (row < 4 * GC) & alone)
    query_mask = queries_mask(rows)
    mixed = []
    units = [(g, hp, i) for g in range(2) for hp in range(features // 128) for i in range(2)]
    scores, weights, loaded, blocks = {}, {}, {}, []
    for t in range(len(units) + LAG + LATE):
        if t < len(units):
            g, hp, i = units[t]
            group = step * 2 + g
            if i == 0:
                mine = group // 4 == core
                turn = lax.rem(group, 4) ^ x

                def gathered(at):
                    glob = jnp.where(mine, own_ref[turn, :, at], other_ref[turn, :, at])
                    return jnp.concatenate([near_ref[group, :, at], far_ref[group, :, at], glob], 0)

                lanes = slice(hp * 128, hp * 128 + 128)
                late = slice(features + hp * 128, features + hp * 128 + 128)
                loaded[g, hp] = q_ref[group, :, lanes], gathered(lanes), gathered(late).T
            query, keys, _ = loaded[g, hp]
            here = low if i == 0 else jnp.logical_not(low)
            scores[t] = scores_of(here, keys, key_mask, query, query_mask)
        if 0 <= t - LAG < len(units):
            g, hp, i = units[t - LAG]
            head = 2 * hp + i
            score = scores.pop(t - LAG)
            before = stats_ref[step * 2 + g, 0, head : head + 1]
            top = jnp.maximum(jnp.max(score, 0, keepdims=True), before)
            weight = jnp.exp2((score - top) * SCALE)
            keep = jnp.exp2((before - top) * SCALE)
            norm = 1.0 / (stats_ref[step * 2 + g, 1, head : head + 1] * keep + jnp.sum(weight, 0, keepdims=True))
            weights[t - LAG] = weight.astype(BF16), norm, keep * norm
        if t >= LAG + LATE:
            g, hp, i = units[t - LAG - LATE]
            head = 2 * hp + i
            weight, norm, keep = weights.pop(t - LAG - LATE)
            values = loaded[g, hp][2][i * HD : i * HD + HD]
            part = jnp.dot(values, weight, preferred_element_type=F32) * norm
            part = part + sums_ref[step * 2 + g, head * HD : head * HD + HD] * keep
            blocks.append(part.astype(BF16))
            if len(blocks) == features // HD:
                mixed.append(jnp.concatenate(blocks, 0).T)
                blocks = []
    update = jnp.dot(jnp.concatenate(mixed, 0), wo_ref[...], preferred_element_type=F32)
    update = update.reshape(2, frames, GC, width)
    update = jnp.concatenate([update[0], update[1]], 1)
    out_ref[:, 0] = (video_ref[:, 0].astype(F32) + update).astype(BF16)


def finish(video, *others):
    frames, _, columns, width = video.shape
    block = pl.BlockSpec((frames, 1, 16, width), lambda i: (0, 0, i, 0))
    return pl.pallas_call(
        finish_kernel,
        grid=(columns // 16,),
        in_specs=[block] + [VMEM] * len(others),
        out_specs=block,
        out_shape=jax.ShapeDtypeStruct(video.shape, BF16),
        compiler_params=pltpu.CompilerParams(vmem_limit_bytes=24 << 20),
        cost_estimate=pl.CostEstimate(flops=4 << 30, bytes_accessed=6 << 20, transcendentals=0),
        name="finish",
    )(video, *others)


def halo_far(value):
    count = lax.axis_size("clip")
    pairs = []
    for c in range(1, count - 1, 2):
        pairs += [(c, c + 1), (c + 1, c)]
    return lax.ppermute(value, "clip", pairs)


def swap_x(value, s):
    return send(value, lambda y, z, x, c: (y, z, x ^ s, c))


def local(video, frame_pick, w_query, w_key, w_value, w_out):
    width = video.shape[-1]
    weights = (w_query, w_key, w_value)
    rows4 = jax.ShapeDtypeStruct((4, width), F32)
    other_core = lambda y, z, x, c: (y, z, x, 1 - c)

    keep, give = pick(video, frame_pick)
    came = send(give, other_core)
    parts = call(split_kernel, [rows4] * 4, "split", [keep, came])
    arrived = [swap_x(parts[s], s) for s in (1, 2, 3)]
    made = qkv(0, video, weights, [], [parts[0]])
    term = call(sum_kernel, rows4, "total", [parts[0], *arrived], [made[2]])
    pair = send(term, lambda y, z, x, c: (y, z ^ 1, x, c))
    made = qkv(1, video, weights, made, [term])
    glob = call(glob_kernel, jax.ShapeDtypeStruct((1, 4, width), BF16), "glob", [term, pair], [made[2]])
    stacked = lambda n: jax.ShapeDtypeStruct((n, 4, width), BF16)
    came = send(glob, lambda y, z, x, c: (y, z ^ 2, x, c))
    made = qkv(2, video, weights, made, [glob])
    glob = call(stack_kernel, stacked(2), "stack2", [glob, came], [made[2]])
    came = send(glob, lambda y, z, x, c: (y, 7 - z, x, c))
    made = qkv(3, video, weights, made, [glob])
    glob = call(stack_kernel, stacked(4), "stack4", [glob, came], [made[2]])
    globs = [glob] + [send(glob, lambda y, z, x, c, s=s: (y ^ s, z, x, c)) for s in (1, 2, 3)]
    q, kv, near, far = made
    done = near_part((0, 1), q, kv, [], [glob])
    piece = call(
        project_kernel,
        jax.ShapeDtypeStruct((1, 64, 2 * w_key.shape[1]), BF16),
        "project",
        [*globs, w_key, w_value],
        [done[1]],
        flops=1 << 28,
    )
    ring = [swap_x(piece, s) for s in (1, 2, 3)]
    near = send(near, other_core)
    far = halo_far(far)
    done = near_part((2, 3, 4, 5, 6, 7), q, kv, done, [piece])
    own = call(
        stack_kernel, jax.ShapeDtypeStruct((4,) + piece.shape[1:], BF16), "own", [piece, *ring], [done[1]]
    )
    other = send(own, other_core)
    return finish(video, q, *done, near, far, own, other, w_out)


def solution(mesh):
    placed = (P("clip", "row", None, None), P("clip"), P(), P(), P(), P())
    return jax.shard_map(
        local, mesh=mesh, in_specs=placed, out_specs=P("clip", "row", None, None), check_vma=False
    )
```

```python
import functools
import math

import jax
import jax.numpy as jnp
from jax import lax
from jax.experimental import pallas as pl
from jax.experimental.pallas import tpu as pltpu
from jax.sharding import PartitionSpec as P

HD = 64
GC = 8
AXES = ("clip", "row")
BIG = -1e30
F32 = jnp.float32
BF16 = jnp.bfloat16


def place(i):
    clip, xh = divmod(i, 2)
    return (clip >> 5, (clip >> 2) & 7, xh * 2 + ((clip >> 1) & 1), clip & 1)


def index(y, z, x, core):
    clip = ((y * 8 + z) * 2 + (x & 1)) * 2 + core
    return clip * 2 + (x >> 1)


def send(value, move):
    pairs = [(i, index(*move(*place(i)))) for i in range(256)]
    return lax.ppermute(value, AXES, pairs)


def layer_norm(values):
    centre = values - jnp.mean(values, -1, keepdims=True)
    spread = jnp.mean(centre * centre, -1, keepdims=True)
    return centre * lax.rsqrt(spread + 1e-05)


def my_place():
    clip = lax.axis_index("clip")
    return lax.axis_index("row") * 2 + lax.rem(clip // 2, 2), lax.rem(clip, 2)


LONG = 2 << 30
PICK = 53
VMEM = pl.BlockSpec(memory_space=pltpu.VMEM)
ANY = pl.BlockSpec(memory_space=pl.ANY)


def call(kernel, out_shape, name, operands, after=(), aliases=None, limit=16, flops=LONG):
    count = len(operands)

    def body(*refs):
        kernel(*refs[:count], *refs[count + len(after) :])

    single = not isinstance(out_shape, (list, tuple))
    return pl.pallas_call(
        body,
        in_specs=[VMEM] * count + [ANY] * len(after),
        out_specs=VMEM if single else [VMEM] * len(out_shape),
        out_shape=out_shape,
        input_output_aliases=aliases or {},
        compiler_params=pltpu.CompilerParams(vmem_limit_bytes=limit << 20),
        cost_estimate=pl.CostEstimate(flops=flops, bytes_accessed=1 << 14, transcendentals=0),
        name=name,
    )(*operands, *after)


def pick_kernel(pick_ref, video_ref, keep_ref, give_ref, near_ref, far_ref, frame_ref, semaphores):
    x, core = my_place()
    last = video_ref.shape[0] - 2
    copy = pltpu.make_async_copy(video_ref.at[pick_ref[0], 0], frame_ref, semaphores.at[0])
    copy.start()
    ends = [
        pltpu.make_async_copy(video_ref.at[pl.ds(start, 2), 0], ref, semaphores.at[i])
        for i, start, ref in ((1, last * (1 - core), near_ref), (2, last * core, far_ref))
    ]
    for end in ends:
        end.start()
    row = lax.broadcasted_iota(jnp.int32, (32, 64), 0)
    column = lax.broadcasted_iota(jnp.int32, (32, 64), 1)
    half = jnp.where(row < 16, core, 1 - core)
    quarter = ((row // 4) % 4) ^ x
    pooled = half * 16 + quarter * 4 + row % 4
    pairs = jnp.where(column // 2 == pooled, 1.0, 0.0).astype(BF16)
    copy.wait()
    normed = layer_norm(frame_ref[...].astype(F32)).astype(BF16)
    term = jnp.dot(pairs, normed, preferred_element_type=F32)
    keep_ref[...] = term[:16]
    give_ref[...] = term[16:]
    for end in ends:
        end.wait()


def pick(video, frame_pick):
    width = video.shape[-1]
    half = jax.ShapeDtypeStruct((16, width), F32)
    ends = jax.ShapeDtypeStruct((2, 64, width), BF16)
    return pl.pallas_call(
        pick_kernel,
        in_specs=[pl.BlockSpec(memory_space=pltpu.SMEM), pl.BlockSpec(memory_space=pltpu.HBM)],
        out_specs=[VMEM] * 4,
        out_shape=[half, half, ends, ends],
        scratch_shapes=[pltpu.VMEM((64, width), BF16), pltpu.SemaphoreType.DMA((3,))],
        compiler_params=pltpu.CompilerParams(vmem_limit_bytes=PICK << 20),
        cost_estimate=pl.CostEstimate(flops=LONG, bytes_accessed=1 << 18, transcendentals=0),
        name="pick",
    )(frame_pick, video)


def split_kernel(keep_ref, came_ref, *out_refs):
    total = keep_ref[...] + came_ref[...]
    for s, out in enumerate(out_refs):
        out[...] = total[4 * s : 4 * s + 4]


def sum_kernel(a_ref, b_ref, c_ref, d_ref, far_ref, out_ref, same_ref):
    out_ref[...] = (a_ref[...] + b_ref[...]) + (c_ref[...] + d_ref[...])


def glob_kernel(a_ref, b_ref, out_ref):
    out_ref[0] = layer_norm(a_ref[...] + b_ref[...]).astype(BF16)


def stack_kernel(*refs):
    out_ref = refs[-1]
    at = 0
    for ref in refs[:-1]:
        out_ref[at : at + ref.shape[0]] = ref[...]
        at += ref.shape[0]


def project_kernel(*refs):
    globs, (wk_ref, wv_ref, out_ref) = refs[:-3], refs[-3:]
    glob = jnp.concatenate([ref[i].astype(F32) for ref in globs for i in range(ref.shape[0])], 0).astype(BF16)
    features = wk_ref.shape[1]
    out_ref[0, :, :features] = jnp.dot(glob, wk_ref[...], preferred_element_type=F32).astype(BF16)
    out_ref[0, :, features:] = jnp.dot(glob, wv_ref[...], preferred_element_type=F32).astype(BF16)


def qkv_kernel(part, *refs):
    video_ref, wq_ref, wk_ref, wv_ref = refs[:4]
    q_ref, kv_ref = refs[-2:]
    width = video_ref.shape[-1]
    features = wq_ref.shape[1]
    normed = layer_norm(video_ref[:, 0, part * 16 : part * 16 + 16].astype(F32))
    normed = jnp.concatenate([normed[:, :GC].reshape(-1, width), normed[:, GC:].reshape(-1, width)], 0)
    normed = normed.astype(BF16)
    rows = normed.shape[0] // 2
    mine = slice(2 * part, 2 * part + 2)
    query = jnp.dot(normed, wq_ref[...], preferred_element_type=F32).astype(BF16)
    q_ref[mine] = query.reshape(2, rows, features)
    for at, w_ref in ((slice(0, features), wk_ref), (slice(features, 2 * features), wv_ref)):
        made = jnp.dot(normed, w_ref[...], preferred_element_type=F32).astype(BF16)
        kv_ref[mine, :, at] = made.reshape(2, rows, features)


def ends_kernel(near_ref, far_ref, wk_ref, wv_ref, *out_refs):
    columns, width = near_ref.shape[1:]
    features = wk_ref.shape[1]
    normed = []
    for ref in (near_ref, far_ref):
        one = layer_norm(ref[...].astype(F32)).reshape(2, columns // GC, GC, width)
        normed.append(jnp.concatenate([one[f, g] for g in range(columns // GC) for f in range(2)], 0))
    normed = jnp.concatenate(normed, 0).astype(BF16)
    rows = 2 * columns
    for at, w_ref in ((slice(0, features), wk_ref), (slice(features, 2 * features), wv_ref)):
        made = jnp.dot(normed, w_ref[...], preferred_element_type=F32).astype(BF16)
        for i, out in enumerate(out_refs):
            out[:, :, at] = made[i * rows : i * rows + rows].reshape(columns // GC, 2 * GC, features)


def qkv(part, video, weights, made, after):
    frames, _, columns, width = video.shape
    features = weights[0].shape[1]
    groups = columns // GC
    sizes = [(frames * GC, features), (frames * GC, 2 * features)]
    return call(
        functools.partial(qkv_kernel, part),
        [jax.ShapeDtypeStruct((groups,) + s, BF16) for s in sizes],
        "qkv",
        [video, *weights, *made],
        after,
        {4 + i: i for i in range(len(made))},
        flops=2 * frames * 16 * width * 3 * features,
    )


LAG, LATE = 8, 4
SCALE = math.log2(math.e) / math.sqrt(HD)


def queries_mask(rows):
    spot = lax.broadcasted_iota(jnp.int32, (rows, 128), 1) % HD
    row = lax.broadcasted_iota(jnp.int32, (rows, 128), 0)
    return jnp.where((spot == row % GC) | (spot == GC), 1.0, 0.0).astype(BF16)


def keys_mask(plain, pooled, absent):
    spot = lax.broadcasted_iota(jnp.int32, (plain + pooled, 128), 1) % HD
    row = lax.broadcasted_iota(jnp.int32, (plain + pooled, 128), 0)
    same = row % GC == spot
    if pooled:
        same = (same & (row < plain)) | ((row % 4 == spot // 2) & (row >= plain))
    bad = (spot < GC) & jnp.logical_not(same)
    if absent is not None:
        bad = bad | ((spot == GC) & absent(row))
    return jnp.where(bad, BIG, 0.0).astype(BF16)


def scores_of(here, keys, key_mask, query, query_mask):
    return lax.dot_general(
        jnp.where(here, keys, key_mask),
        jnp.where(here, query, query_mask),
        (((1,), (1,)), ((), ())),
        preferred_element_type=F32,
    )


def near_kernel(groups, *refs):
    q_ref, kv_ref, near_ref, far_ref = refs[:4]
    sums_ref, stats_ref = refs[-2:]
    rows, features = q_ref.shape[1:]
    clip = lax.axis_index("clip")
    alone = (clip == 0) | (clip == lax.axis_size("clip") - 1)
    low = lax.broadcasted_iota(jnp.int32, (1, 128), 1) < HD
    key_mask = keys_mask(rows + 4 * GC, 0, lambda row: (row >= rows + 2 * GC) & alone)
    query_mask = queries_mask(rows)

    def gathered(g, at):
        return jnp.concatenate([kv_ref[g, :, at], near_ref[g, :, at], far_ref[g, :, at]], 0)

    units = [(g, hp, i) for g in groups for hp in range(features // 128) for i in range(2)]
    scores, weights, loaded = {}, {}, {}
    for t in range(len(units) + LAG + LATE):
        if t < len(units):
            g, hp, i = units[t]
            if i == 0:
                lanes = slice(hp * 128, hp * 128 + 128)
                late = slice(features + hp * 128, features + hp * 128 + 128)
                loaded[g, hp] = q_ref[g, :, lanes], gathered(g, lanes), gathered(g, late).T
            query, keys, _ = loaded[g, hp]
            here = low if i == 0 else jnp.logical_not(low)
            scores[t] = scores_of(here, keys, key_mask, query, query_mask)
        if 0 <= t - LAG < len(units):
            g, hp, i = units[t - LAG]
            score = scores.pop(t - LAG)
            top = jnp.max(score, 0, keepdims=True)
            weight = jnp.exp2((score - top) * SCALE)
            head = 2 * hp + i
            stats_ref[g, 0, head : head + 1] = top
            stats_ref[g, 1, head : head + 1] = jnp.sum(weight, 0, keepdims=True)
            weights[t - LAG] = weight.astype(BF16)
        if t >= LAG + LATE:
            g, hp, i = units[t - LAG - LATE]
            head = 2 * hp + i
            values = loaded[g, hp][2][i * HD : i * HD + HD]
            sums_ref[g, head * HD : head * HD + HD] = jnp.dot(
                values, weights.pop(t - LAG - LATE), preferred_element_type=F32
            )


def near_part(groups, q, kv, near, far, w_out, made, after):
    count, rows, features = q.shape
    return call(
        functools.partial(near_kernel, groups),
        [
            jax.ShapeDtypeStruct((count, features, rows), F32),
            jax.ShapeDtypeStruct((count, 2, 16, rows), F32),
        ],
        "near",
        [q, kv, near, far, w_out, *made],
        after,
        {5 + i: i for i in range(len(made))},
        flops=len(groups) * 300 << 20,
    )


def finish_kernel(mine, video_ref, q_ref, sums_ref, stats_ref, glob_ref, wo_ref, *refs):
    out_ref, made_ref, semaphores = refs[-3:]
    frames, _, _, width = video_ref.shape
    rows, features = q_ref.shape[1:]
    heads = features // HD
    x, core = my_place()
    first = (core if mine else 1 - core) * 2
    low = lax.broadcasted_iota(jnp.int32, (1, 128), 1) < HD
    key_mask = keys_mask(0, 64, None)
    query_mask = queries_mask(rows)
    units = [(p, g, hp, i) for p in range(2) for g in range(2) for hp in range(features // 128) for i in range(2)]
    scores, weights, loaded, blocks, mixed = {}, {}, {}, [], []
    attended, waiting, copies = {}, [], []

    def columns_of(p):
        return pl.ds(pl.multiple_of((first + p) * 16, 16), 16)

    def project_out(p, part):
        at = slice(part * 256, part * 256 + 256)
        update = jnp.dot(attended[p], wo_ref[:, at], preferred_element_type=F32)
        update = update.reshape(2, frames, GC, 256)
        update = jnp.concatenate([update[0], update[1]], 1)
        made_ref[p, :, :, at] = (video_ref[:, 0, columns_of(p), at].astype(F32) + update).astype(BF16)
        if part == width // 256 - 1:
            copy = pltpu.make_async_copy(made_ref.at[p], out_ref.at[:, 0, columns_of(p)], semaphores.at[p])
            copy.start()
            copies.append(copy)

    for t in range(len(units) + LAG + LATE):
        if t < len(units):
            p, g, hp, i = units[t]
            group = (first + p) * 2 + g
            if i == 0:
                turn = lax.rem(group, 4) ^ x
                lanes = slice(hp * 128, hp * 128 + 128)
                late = slice(features + hp * 128, features + hp * 128 + 128)
                loaded[p, g, hp] = q_ref[group, :, lanes], glob_ref[turn, :, lanes], glob_ref[turn, :, late].T
            query, keys, _ = loaded[p, g, hp]
            here = low if i == 0 else jnp.logical_not(low)
            scores[t] = scores_of(here, keys, key_mask, query, query_mask)
        if 0 <= t - LAG < len(units):
            p, g, hp, i = units[t - LAG]
            group, head = (first + p) * 2 + g, 2 * hp + i
            score = scores.pop(t - LAG)
            before = stats_ref[group, 0, head : head + 1]
            top = jnp.maximum(jnp.max(score, 0, keepdims=True), before)
            weight = jnp.exp2((score - top) * SCALE)
            keep = jnp.exp2((before - top) * SCALE)
            norm = 1.0 / (stats_ref[group, 1, head : head + 1] * keep + jnp.sum(weight, 0, keepdims=True))
            weights[t - LAG] = weight.astype(BF16), norm, keep * norm
        if t >= LAG + LATE:
            p, g, hp, i = units[t - LAG - LATE]
            group, head = (first + p) * 2 + g, 2 * hp + i
            weight, norm, keep = weights.pop(t - LAG - LATE)
            values = loaded[p, g, hp][2][i * HD : i * HD + HD]
            part = jnp.dot(values, weight, preferred_element_type=F32) * norm
            part = part + sums_ref[group, head * HD : head * HD + HD] * keep
            blocks.append(part.astype(BF16))
            if len(blocks) == heads:
                mixed.append(jnp.concatenate(blocks, 0).T)
                blocks = []
            if len(mixed) == 2:
                attended[p] = jnp.concatenate(mixed, 0)
                waiting += [(p, part) for part in range(width // 256)]
                mixed = []
            elif waiting and i == 1:
                project_out(*waiting.pop(0))
    for job in waiting:
        project_out(*job)
    for copy in copies:
        copy.wait()


def finish(mine, video, q, sums, stats, glob, w_out, made):
    frames, _, _, width = video.shape
    operands = [video, q, sums, stats, glob, w_out]
    return pl.pallas_call(
        functools.partial(finish_kernel, mine),
        in_specs=[VMEM] * len(operands) + [ANY] * len(made),
        out_specs=ANY,
        out_shape=jax.ShapeDtypeStruct(video.shape, BF16),
        input_output_aliases={len(operands): 0} if made else {},
        scratch_shapes=[pltpu.VMEM((2, frames, 16, width), BF16), pltpu.SemaphoreType.DMA((2,))],
        compiler_params=pltpu.CompilerParams(vmem_limit_bytes=24 << 20),
        cost_estimate=pl.CostEstimate(flops=2 << 30, bytes_accessed=6 << 20, transcendentals=0),
        name="finish",
    )(*operands, *made)


def halo_far(value):
    count = lax.axis_size("clip")
    pairs = []
    for c in range(1, count - 1, 2):
        pairs += [(c, c + 1), (c + 1, c)]
    return lax.ppermute(value, "clip", pairs)


def swap_x(value, s):
    return send(value, lambda y, z, x, c: (y, z, x ^ s, c))


def local(video, frame_pick, w_query, w_key, w_value, w_out):
    width = video.shape[-1]
    weights = (w_query, w_key, w_value)
    rows4 = jax.ShapeDtypeStruct((4, width), F32)
    other_core = lambda y, z, x, c: (y, z, x, 1 - c)

    keep, give, near, far = pick(video, frame_pick)
    came = send(give, other_core)
    parts = call(split_kernel, [rows4] * 4, "split", [keep, came], flops=3 * LONG)
    arrived = [swap_x(parts[s], s) for s in (1, 2, 3)]
    made = qkv(0, video, weights, [], [parts[0]])
    near = send(near, other_core)
    term, far = call(
        sum_kernel,
        [rows4, jax.ShapeDtypeStruct(far.shape, BF16)],
        "total",
        [parts[0], *arrived, far],
        [made[1], near],
        {4: 1},
        flops=1 << 20,
    )
    pair = send(term, lambda y, z, x, c: (y, z ^ 1, x, c))
    far = halo_far(far)
    glob = call(glob_kernel, jax.ShapeDtypeStruct((1, 4, width), BF16), "glob", [term, pair])
    stacked = lambda n: jax.ShapeDtypeStruct((n, 4, width), BF16)
    came = send(glob, lambda y, z, x, c: (y, z ^ 2, x, c))
    made = qkv(1, video, weights, made, [glob])
    glob = call(stack_kernel, stacked(2), "stack2", [glob, came], [made[1]])
    came = send(glob, lambda y, z, x, c: (y, 7 - z, x, c))
    made = qkv(2, video, weights, made, [glob])
    glob = call(stack_kernel, stacked(4), "stack4", [glob, came], [made[1], far])
    globs = [glob] + [send(glob, lambda y, z, x, c, s=s: (y ^ s, z, x, c)) for s in (1, 2, 3)]
    q, kv = qkv(3, video, weights, made, [glob])
    side = jax.ShapeDtypeStruct((video.shape[2] // GC, 2 * GC, 2 * w_key.shape[1]), BF16)
    near, far = call(ends_kernel, [side, side], "ends", [near, far, w_key, w_value], [kv])
    piece = call(
        project_kernel,
        jax.ShapeDtypeStruct((1, 64, 2 * w_key.shape[1]), BF16),
        "project",
        [*globs, w_key, w_value],
        [far],
        flops=1 << 28,
    )
    ring = [swap_x(piece, s) for s in (1, 2, 3)]
    done = near_part(range(8), q, kv, near, far, w_out, [], [piece])
    own = call(
        stack_kernel, jax.ShapeDtypeStruct((4,) + piece.shape[1:], BF16), "own", [piece, *ring], [done[1]]
    )
    other = send(own, other_core)
    mixed = finish(True, video, q, *done, own, w_out, [])
    return finish(False, video, q, *done, other, w_out, [mixed])


def solution(mesh):
    placed = (P("clip", "row", None, None), P("clip"), P(), P(), P(), P())
    return jax.shard_map(
        local, mesh=mesh, in_specs=placed, out_specs=P("clip", "row", None, None), check_vma=False
    )
```

```python
import functools
import math

import jax
import jax.numpy as jnp
from jax import lax
from jax.experimental import pallas as pl
from jax.experimental.pallas import tpu as pltpu
from jax.sharding import PartitionSpec as P

HD = 64
GC = 8
AXES = ("clip", "row")
BIG = -1e30
F32 = jnp.float32
BF16 = jnp.bfloat16


def place(i):
    clip, xh = divmod(i, 2)
    return (clip >> 5, (clip >> 2) & 7, xh * 2 + ((clip >> 1) & 1), clip & 1)


def index(y, z, x, core):
    clip = ((y * 8 + z) * 2 + (x & 1)) * 2 + core
    return clip * 2 + (x >> 1)


def send(value, move):
    pairs = [(i, index(*move(*place(i)))) for i in range(256)]
    return lax.ppermute(value, AXES, pairs)


def layer_norm(values):
    centre = values - jnp.mean(values, -1, keepdims=True)
    spread = jnp.mean(centre * centre, -1, keepdims=True)
    return centre * lax.rsqrt(spread + 1e-05)


def my_place():
    clip = lax.axis_index("clip")
    return lax.axis_index("row") * 2 + lax.rem(clip // 2, 2), lax.rem(clip, 2)


LONG = 2 << 30
PICK = 53
VMEM = pl.BlockSpec(memory_space=pltpu.VMEM)
ANY = pl.BlockSpec(memory_space=pl.ANY)


def call(kernel, out_shape, name, operands, after=(), aliases=None, limit=16, flops=LONG):
    count = len(operands)

    def body(*refs):
        kernel(*refs[:count], *refs[count + len(after) :])

    single = not isinstance(out_shape, (list, tuple))
    return pl.pallas_call(
        body,
        in_specs=[VMEM] * count + [ANY] * len(after),
        out_specs=VMEM if single else [VMEM] * len(out_shape),
        out_shape=out_shape,
        input_output_aliases=aliases or {},
        compiler_params=pltpu.CompilerParams(vmem_limit_bytes=limit << 20),
        cost_estimate=pl.CostEstimate(flops=flops, bytes_accessed=1 << 14, transcendentals=0),
        name=name,
    )(*operands, *after)


def pick_kernel(pick_ref, video_ref, keep_ref, give_ref, near_ref, far_ref, frame_ref, semaphores):
    x, core = my_place()
    last = video_ref.shape[0] - 2
    copy = pltpu.make_async_copy(video_ref.at[pick_ref[0], 0], frame_ref, semaphores.at[0])
    copy.start()
    ends = [
        pltpu.make_async_copy(video_ref.at[pl.ds(start, 2), 0], ref, semaphores.at[i])
        for i, start, ref in ((1, last * (1 - core), near_ref), (2, last * core, far_ref))
    ]
    for end in ends:
        end.start()
    row = lax.broadcasted_iota(jnp.int32, (32, 64), 0)
    column = lax.broadcasted_iota(jnp.int32, (32, 64), 1)
    half = jnp.where(row < 16, core, 1 - core)
    quarter = ((row // 4) % 4) ^ x
    pooled = half * 16 + quarter * 4 + row % 4
    pairs = jnp.where(column // 2 == pooled, 1.0, 0.0).astype(BF16)
    copy.wait()
    normed = layer_norm(frame_ref[...].astype(F32)).astype(BF16)
    term = jnp.dot(pairs, normed, preferred_element_type=F32)
    keep_ref[...] = term[:16]
    give_ref[...] = term[16:]
    for end in ends:
        end.wait()


def pick(video, frame_pick):
    width = video.shape[-1]
    half = jax.ShapeDtypeStruct((16, width), F32)
    ends = jax.ShapeDtypeStruct((2, 64, width), BF16)
    return pl.pallas_call(
        pick_kernel,
        in_specs=[pl.BlockSpec(memory_space=pltpu.SMEM), pl.BlockSpec(memory_space=pltpu.HBM)],
        out_specs=[VMEM] * 4,
        out_shape=[half, half, ends, ends],
        scratch_shapes=[pltpu.VMEM((64, width), BF16), pltpu.SemaphoreType.DMA((3,))],
        compiler_params=pltpu.CompilerParams(vmem_limit_bytes=PICK << 20),
        cost_estimate=pl.CostEstimate(flops=LONG, bytes_accessed=1 << 18, transcendentals=0),
        name="pick",
    )(frame_pick, video)


def split_kernel(keep_ref, came_ref, *out_refs):
    total = keep_ref[...] + came_ref[...]
    for s, out in enumerate(out_refs):
        out[...] = total[4 * s : 4 * s + 4]


def sum_kernel(a_ref, b_ref, c_ref, d_ref, far_ref, out_ref, same_ref):
    out_ref[...] = (a_ref[...] + b_ref[...]) + (c_ref[...] + d_ref[...])


def glob_kernel(a_ref, b_ref, out_ref):
    out_ref[0] = layer_norm(a_ref[...] + b_ref[...]).astype(BF16)


def stack_kernel(*refs):
    out_ref = refs[-1]
    at = 0
    for ref in refs[:-1]:
        out_ref[at : at + ref.shape[0]] = ref[...]
        at += ref.shape[0]


def project_kernel(*refs):
    globs, (wk_ref, wv_ref, out_ref) = refs[:-3], refs[-3:]
    glob = jnp.concatenate([ref[i].astype(F32) for ref in globs for i in range(ref.shape[0])], 0).astype(BF16)
    features = wk_ref.shape[1]
    out_ref[0, :, :features] = jnp.dot(glob, wk_ref[...], preferred_element_type=F32).astype(BF16)
    out_ref[0, :, features:] = jnp.dot(glob, wv_ref[...], preferred_element_type=F32).astype(BF16)


def qkv_kernel(part, *refs):
    video_ref, wq_ref, wk_ref, wv_ref = refs[:4]
    q_ref, kv_ref = refs[-2:]
    width = video_ref.shape[-1]
    features = wq_ref.shape[1]
    normed = layer_norm(video_ref[:, 0, part * 16 : part * 16 + 16].astype(F32))
    normed = jnp.concatenate([normed[:, :GC].reshape(-1, width), normed[:, GC:].reshape(-1, width)], 0)
    normed = normed.astype(BF16)
    rows = normed.shape[0] // 2
    mine = slice(2 * part, 2 * part + 2)
    query = jnp.dot(normed, wq_ref[...], preferred_element_type=F32).astype(BF16)
    q_ref[mine] = query.reshape(2, rows, features)
    for at, w_ref in ((slice(0, features), wk_ref), (slice(features, 2 * features), wv_ref)):
        made = jnp.dot(normed, w_ref[...], preferred_element_type=F32).astype(BF16)
        kv_ref[mine, :, at] = made.reshape(2, rows, features)


def ends_kernel(near_ref, far_ref, wk_ref, wv_ref, *out_refs):
    columns, width = near_ref.shape[1:]
    features = wk_ref.shape[1]
    normed = []
    for ref in (near_ref, far_ref):
        one = layer_norm(ref[...].astype(F32)).reshape(2, columns // GC, GC, width)
        normed.append(jnp.concatenate([one[f, g] for g in range(columns // GC) for f in range(2)], 0))
    normed = jnp.concatenate(normed, 0).astype(BF16)
    rows = 2 * columns
    for at, w_ref in ((slice(0, features), wk_ref), (slice(features, 2 * features), wv_ref)):
        made = jnp.dot(normed, w_ref[...], preferred_element_type=F32).astype(BF16)
        for i, out in enumerate(out_refs):
            out[:, :, at] = made[i * rows : i * rows + rows].reshape(columns // GC, 2 * GC, features)


def qkv(part, video, weights, made, after):
    frames, _, columns, width = video.shape
    features = weights[0].shape[1]
    groups = columns // GC
    sizes = [(frames * GC, features), (frames * GC, 2 * features)]
    return call(
        functools.partial(qkv_kernel, part),
        [jax.ShapeDtypeStruct((groups,) + s, BF16) for s in sizes],
        "qkv",
        [video, *weights, *made],
        after,
        {4 + i: i for i in range(len(made))},
        flops=2 * frames * 16 * width * 3 * features,
    )


LAG, LATE = 8, 4
SCALE = math.log2(math.e) / math.sqrt(HD)


def queries_mask(rows):
    spot = lax.broadcasted_iota(jnp.int32, (rows, 128), 1) % HD
    row = lax.broadcasted_iota(jnp.int32, (rows, 128), 0)
    return jnp.where((spot == row % GC) | (spot == GC), 1.0, 0.0).astype(BF16)


def keys_mask(plain, pooled, absent):
    spot = lax.broadcasted_iota(jnp.int32, (plain + pooled, 128), 1) % HD
    row = lax.broadcasted_iota(jnp.int32, (plain + pooled, 128), 0)
    same = row % GC == spot
    if pooled:
        same = (same & (row < plain)) | ((row % 4 == spot // 2) & (row >= plain))
    bad = (spot < GC) & jnp.logical_not(same)
    if absent is not None:
        bad = bad | ((spot == GC) & absent(row))
    return jnp.where(bad, BIG, 0.0).astype(BF16)


def scores_of(here, keys, key_mask, query, query_mask):
    return lax.dot_general(
        jnp.where(here, keys, key_mask),
        jnp.where(here, query, query_mask),
        (((1,), (1,)), ((), ())),
        preferred_element_type=F32,
    )


def near_kernel(groups, *refs):
    q_ref, kv_ref, near_ref, far_ref = refs[:4]
    sums_ref, stats_ref = refs[-2:]
    rows, features = q_ref.shape[1:]
    clip = lax.axis_index("clip")
    alone = (clip == 0) | (clip == lax.axis_size("clip") - 1)
    low = lax.broadcasted_iota(jnp.int32, (1, 128), 1) < HD
    key_mask = keys_mask(rows + 4 * GC, 0, lambda row: (row >= rows + 2 * GC) & alone)
    query_mask = queries_mask(rows)

    def gathered(g, at):
        return jnp.concatenate([kv_ref[g, :, at], near_ref[g, :, at], far_ref[g, :, at]], 0)

    units = [(g, hp, i) for g in groups for hp in range(features // 128) for i in range(2)]
    scores, weights, loaded = {}, {}, {}
    for t in range(len(units) + LAG + LATE):
        if t < len(units):
            g, hp, i = units[t]
            if i == 0:
                lanes = slice(hp * 128, hp * 128 + 128)
                late = slice(features + hp * 128, features + hp * 128 + 128)
                loaded[g, hp] = q_ref[g, :, lanes], gathered(g, lanes), gathered(g, late).T
            query, keys, _ = loaded[g, hp]
            here = low if i == 0 else jnp.logical_not(low)
            scores[t] = scores_of(here, keys, key_mask, query, query_mask)
        if 0 <= t - LAG < len(units):
            g, hp, i = units[t - LAG]
            score = scores.pop(t - LAG)
            top = jnp.max(score, 0, keepdims=True)
            weight = jnp.exp2((score - top) * SCALE)
            head = 2 * hp + i
            stats_ref[g, 0, head : head + 1] = top
            stats_ref[g, 1, head : head + 1] = jnp.sum(weight, 0, keepdims=True)
            weights[t - LAG] = weight.astype(BF16)
        if t >= LAG + LATE:
            g, hp, i = units[t - LAG - LATE]
            head = 2 * hp + i
            values = loaded[g, hp][2][i * HD : i * HD + HD]
            sums_ref[g, head * HD : head * HD + HD] = jnp.dot(
                values, weights.pop(t - LAG - LATE), preferred_element_type=F32
            )


def near_part(groups, q, kv, near, far, w_out, made, after):
    count, rows, features = q.shape
    return call(
        functools.partial(near_kernel, groups),
        [
            jax.ShapeDtypeStruct((count, features, rows), F32),
            jax.ShapeDtypeStruct((count, 2, 16, rows), F32),
        ],
        "near",
        [q, kv, near, far, w_out, *made],
        after,
        {5 + i: i for i in range(len(made))},
        flops=len(groups) * 300 << 20,
    )


def finish_kernel(mine, video_ref, q_ref, sums_ref, stats_ref, glob_ref, wo_ref, *refs):
    carried_ref = refs[1 if mine else 0]
    out_ref = refs[0] if mine else refs[-3]
    made_ref, semaphores = refs[-2:]
    frames, _, _, width = video_ref.shape
    rows, features = q_ref.shape[1:]
    heads = features // HD
    x, core = my_place()
    first = (core if mine else 1 - core) * 2
    low = lax.broadcasted_iota(jnp.int32, (1, 128), 1) < HD
    key_mask = keys_mask(0, 64, None)
    query_mask = queries_mask(rows)
    units = [(p, g, hp, i) for p in range(2) for g in range(2) for hp in range(features // 128) for i in range(2)]
    scores, weights, loaded, blocks, mixed = {}, {}, {}, [], []
    attended, waiting, copies = {}, [], []
    if not mine:
        attended[2] = carried_ref[...]
        waiting += [(2, part) for part in range(width // 256)]

    def columns_of(p):
        return pl.ds(pl.multiple_of((core * 2 + 1 if p == 2 else first + p) * 16, 16), 16)

    def copy_out(p, at, index):
        copy = pltpu.make_async_copy(made_ref.at[p, at], out_ref.at[at, 0, columns_of(p)], semaphores.at[index])
        copy.start()
        copies.append(copy)

    def project_out(p, part):
        at = slice(part * 256, part * 256 + 256)
        update = jnp.dot(attended[p], wo_ref[:, at], preferred_element_type=F32)
        update = update.reshape(2, frames, GC, 256)
        update = jnp.concatenate([update[0], update[1]], 1)
        made_ref[p, :, :, at] = (video_ref[:, 0, columns_of(p), at].astype(F32) + update).astype(BF16)
        if part == width // 256 - 1:
            copy_out(p, pl.ds(0, frames), p)

    def project_half(p, half):
        some = frames // 2
        at = slice(half * some, half * some + some)
        block = attended[p].reshape(2, frames * GC, features)[:, half * some * GC : (half + 1) * some * GC]
        update = jnp.dot(block.reshape(-1, features), wo_ref[...], preferred_element_type=F32)
        update = update.reshape(2, some, GC, width)
        update = jnp.concatenate([update[0], update[1]], 1)
        made_ref[p, at] = (video_ref[at, 0, columns_of(p)].astype(F32) + update).astype(BF16)
        copy_out(p, pl.ds(half * some, some), 3 if half else p)

    for t in range(len(units) + LAG + LATE):
        if t < len(units):
            p, g, hp, i = units[t]
            group = (first + p) * 2 + g
            if i == 0:
                turn = lax.rem(group, 4) ^ x
                lanes = slice(hp * 128, hp * 128 + 128)
                late = slice(features + hp * 128, features + hp * 128 + 128)
                loaded[p, g, hp] = q_ref[group, :, lanes], glob_ref[turn, :, lanes], glob_ref[turn, :, late].T
            query, keys, _ = loaded[p, g, hp]
            here = low if i == 0 else jnp.logical_not(low)
            scores[t] = scores_of(here, keys, key_mask, query, query_mask)
        if 0 <= t - LAG < len(units):
            p, g, hp, i = units[t - LAG]
            group, head = (first + p) * 2 + g, 2 * hp + i
            score = scores.pop(t - LAG)
            before = stats_ref[group, 0, head : head + 1]
            top = jnp.maximum(jnp.max(score, 0, keepdims=True), before)
            weight = jnp.exp2((score - top) * SCALE)
            keep = jnp.exp2((before - top) * SCALE)
            norm = 1.0 / (stats_ref[group, 1, head : head + 1] * keep + jnp.sum(weight, 0, keepdims=True))
            weights[t - LAG] = weight.astype(BF16), norm, keep * norm
        if t >= LAG + LATE:
            p, g, hp, i = units[t - LAG - LATE]
            group, head = (first + p) * 2 + g, 2 * hp + i
            weight, norm, keep = weights.pop(t - LAG - LATE)
            values = loaded[p, g, hp][2][i * HD : i * HD + HD]
            part = jnp.dot(values, weight, preferred_element_type=F32) * norm
            part = part + sums_ref[group, head * HD : head * HD + HD] * keep
            blocks.append(part.astype(BF16))
            if len(blocks) == heads:
                mixed.append(jnp.concatenate(blocks, 0).T)
                blocks = []
            if len(mixed) == 2:
                attended[p] = jnp.concatenate(mixed, 0)
                mixed = []
                if p == 0:
                    waiting += [(p, part) for part in range(width // 256)]
            elif waiting and i == 1:
                project_out(*waiting.pop(0))
    for job in waiting:
        project_out(*job)
    if mine:
        carried_ref[...] = attended[1]
    else:
        for half in range(2):
            project_half(1, half)
    for copy in copies:
        copy.wait()


def finish(mine, video, q, sums, stats, glob, w_out, made):
    frames, _, _, width = video.shape
    operands = [video, q, sums, stats, glob, w_out]
    whole = jax.ShapeDtypeStruct(video.shape, BF16)
    carried = jax.ShapeDtypeStruct((2 * frames * GC, q.shape[2]), BF16)
    return pl.pallas_call(
        functools.partial(finish_kernel, mine),
        in_specs=[VMEM] * len(operands) + ([] if mine else [VMEM, ANY]),
        out_specs=[ANY, VMEM] if mine else ANY,
        out_shape=[whole, carried] if mine else whole,
        input_output_aliases={} if mine else {len(operands) + 1: 0},
        scratch_shapes=[pltpu.VMEM((3, frames, 16, width), BF16), pltpu.SemaphoreType.DMA((4,))],
        compiler_params=pltpu.CompilerParams(vmem_limit_bytes=24 << 20),
        cost_estimate=pl.CostEstimate(flops=2 << 30, bytes_accessed=6 << 20, transcendentals=0),
        name="finish",
    )(*operands, *made)


def halo_far(value):
    count = lax.axis_size("clip")
    pairs = []
    for c in range(1, count - 1, 2):
        pairs += [(c, c + 1), (c + 1, c)]
    return lax.ppermute(value, "clip", pairs)


def swap_x(value, s):
    return send(value, lambda y, z, x, c: (y, z, x ^ s, c))


def local(video, frame_pick, w_query, w_key, w_value, w_out):
    width = video.shape[-1]
    weights = (w_query, w_key, w_value)
    rows4 = jax.ShapeDtypeStruct((4, width), F32)
    other_core = lambda y, z, x, c: (y, z, x, 1 - c)

    keep, give, near, far = pick(video, frame_pick)
    came = send(give, other_core)
    parts = call(split_kernel, [rows4] * 4, "split", [keep, came], flops=3 * LONG)
    arrived = [swap_x(parts[s], s) for s in (1, 2, 3)]
    made = qkv(0, video, weights, [], [parts[0]])
    near = send(near, other_core)
    term, far = call(
        sum_kernel,
        [rows4, jax.ShapeDtypeStruct(far.shape, BF16)],
        "total",
        [parts[0], *arrived, far],
        [made[1], near],
        {4: 1},
        flops=1 << 20,
    )
    pair = send(term, lambda y, z, x, c: (y, z ^ 1, x, c))
    far = halo_far(far)
    glob = call(glob_kernel, jax.ShapeDtypeStruct((1, 4, width), BF16), "glob", [term, pair])
    stacked = lambda n: jax.ShapeDtypeStruct((n, 4, width), BF16)
    came = send(glob, lambda y, z, x, c: (y, z ^ 2, x, c))
    made = qkv(1, video, weights, made, [glob])
    glob = call(stack_kernel, stacked(2), "stack2", [glob, came], [made[1]])
    came = send(glob, lambda y, z, x, c: (y, 7 - z, x, c))
    glob = call(stack_kernel, stacked(4), "stack4", [glob, came], [far])
    globs = [glob] + [send(glob, lambda y, z, x, c, s=s: (y ^ s, z, x, c)) for s in (1, 2, 3)]
    made = qkv(2, video, weights, made, [glob])
    side = jax.ShapeDtypeStruct((video.shape[2] // GC, 2 * GC, 2 * w_key.shape[1]), BF16)
    near, far = call(ends_kernel, [side, side], "ends", [near, far, w_key, w_value], [made[1]])
    piece = call(
        project_kernel,
        jax.ShapeDtypeStruct((1, 64, 2 * w_key.shape[1]), BF16),
        "project",
        [*globs, w_key, w_value],
        [far],
        flops=1 << 28,
    )
    ring = [swap_x(piece, s) for s in (1, 2, 3)]
    q, kv = qkv(3, video, weights, made, [piece])
    done = near_part(range(8), q, kv, near, far, w_out, [], [piece])
    own = call(
        stack_kernel, jax.ShapeDtypeStruct((4,) + piece.shape[1:], BF16), "own", [piece, *ring], [done[1]]
    )
    other = send(own, other_core)
    mixed, carried = finish(True, video, q, *done, own, w_out, [])
    return finish(False, video, q, *done, other, w_out, [carried, mixed])


def solution(mesh):
    placed = (P("clip", "row", None, None), P("clip"), P(), P(), P(), P())
    return jax.shard_map(
        local, mesh=mesh, in_specs=placed, out_specs=P("clip", "row", None, None), check_vma=False
    )
```
